512 devices in a mesh: row: 16 (over y, core), col: 8 (over z), depth: 4 (over x).
Axes of the slice: x: 4, y: 8, z: 8, core: 2. Of those that a mesh axis runs over, the one named last changes fastest.
Arguments:
- panel_block: float32 [65536, 512], P(('row', 'depth'), 'col'), may hold values from -1 to 1
- trailing: float32 [65536, 4096], P(('row', 'depth'), 'col'), may hold values from -6 to 6
Outputs:
- upper_factor: float32 [512, 512], P(('row', 'depth'))
- coefficients: float32 [512, 4096], P(('row', 'depth'), 'col')
- remainder: float32 [65536, 4096], P(('row', 'depth'), 'col')
The draws below stay inside these ranges and needn't reach their ends.
All inputs are finite; a program needn't handle non-finite values.
Results may differ from the reference program's by a relative error of at most 0.00013.
Values sent between devices are 32-bit elements; how exact they have to be, the bound alone decides.
No kernel may reach another device: no remote copies, remote signals or barrier semaphores. Data moves between devices by JAX's collectives and lax.ppermute only.
A program may use at most 64 MiB of HBM per device.

```python
import math
import jax
import jax.numpy as jnp
from jax import lax

B = 512
NT = 4096
ROWS = 65536


def draw_panel_block(key, part):
    key = jax.random.fold_in(key, 7)
    keys = jax.random.split(key, 4)
    col_scale = jnp.exp(jax.random.uniform(keys[0], (1, B), jnp.float32, 0.0, math.log(4.0)))
    row_scale = jnp.exp(jax.random.uniform(keys[1], (ROWS, 1), jnp.float32, 0.0, math.log(3.0)))
    shared = jax.random.normal(keys[2], (ROWS, 1), jnp.float32)
    base = jax.random.normal(keys[3], (ROWS, B), jnp.float32)
    weight_shared = 0.15
    values = row_scale * (base + weight_shared * shared) * col_scale / math.sqrt(ROWS)
    return jnp.clip(values, -1.0, 1.0).astype(jnp.float32)


def shard_levels(key, shape, cuts, smallest, top_value):
    def one(position, shards_of):
        draws = jax.random.uniform(jax.random.fold_in(jax.random.fold_in(key, 6), position), (shards_of,), jnp.float32, smallest / len(cuts), top_value / len(cuts))
        return jnp.repeat(jnp.exp(draws), shape[position] // shards_of).reshape((-1,) + (1,) * (len(shape) - position - 1))

    loudness = one(*cuts[0])
    for cut in cuts[1:]:
        loudness = loudness * one(*cut)
    return loudness


def gaussian(key, dims, deviation, limit, shards=(), kind=jnp.bfloat16):
    result = deviation * jax.random.normal(key, dims, jnp.float32)
    if shards:
        result = result * shard_levels(key, dims, shards, -0.22, 0.18)
    return jnp.clip(result, -limit, limit).astype(kind)


def setup_inputs(seed: int = 0) -> dict:
    streams_of = jax.random.split(jax.random.key(seed), 3)
    panel_block = draw_panel_block(jax.random.fold_in(streams_of[2], 71), 0)
    trailing = gaussian(streams_of[1], (ROWS, NT), 1.0, 6.0, ((0, 64), (1, 8)), jnp.float32)
    return dict(panel_block=panel_block, trailing=trailing)


def reference(panel_block, trailing):
    exact = lax.Precision.HIGHEST
    gram_matrix = jnp.dot(panel_block.T.astype(jnp.float32), panel_block.astype(jnp.float32), precision=exact, preferred_element_type=jnp.float32)
    lower_factor = jnp.linalg.cholesky(gram_matrix)
    basis_rows = jax.scipy.linalg.solve_triangular(lower_factor, panel_block.T, lower=True)
    coefficients = jnp.dot(basis_rows.astype(jnp.float32), trailing.astype(jnp.float32), precision=exact, preferred_element_type=jnp.float32)
    remainder = trailing - jnp.dot(basis_rows.T.astype(jnp.float32), coefficients.astype(jnp.float32), precision=exact, preferred_element_type=jnp.float32)
    return (lower_factor.T, coefficients, remainder)
```

```python
import functools

import jax
import jax.numpy as jnp
from jax import lax
from jax.experimental import pallas as pl
from jax.experimental.pallas import tpu as pltpu
from jax.sharding import Mesh, PartitionSpec as P

BLOCK = 128
GROUP = 8
PLANE = ("y", "depth")
ROWS = ("y", "core", "depth")
VMEM = pl.BlockSpec(memory_space=pltpu.VMEM)
SMEM = pl.BlockSpec(memory_space=pltpu.SMEM)
ANYWHERE = pl.BlockSpec(memory_space=pl.ANY)
LAST = ((1,), (1,))
FIRST = ((0,), (0,))


def dot(a, b, contract=((1,), (0,))):
    return lax.dot_general(
        a, b, (contract, ((), ())), precision=lax.Precision.HIGHEST, preferred_element_type=jnp.float32
    )


def f32(*shape):
    return jax.ShapeDtypeStruct(shape, jnp.float32)


def params(mib):
    return pltpu.CompilerParams(vmem_limit_bytes=mib * 2**20)


def cost(flops, values):
    return pl.CostEstimate(flops=flops, bytes_accessed=4 * values, transcendentals=0)


def gram_kernel(place_ref, rows_ref, mine_ref, theirs_ref):
    n = rows_ref.shape[0]
    half, quarter = n // 2, n // 4
    top = rows_ref[:half]
    for core, out_ref in ((place_ref[1], mine_ref), (1 - place_ref[1], theirs_ref)):
        block = rows_ref[pl.ds(pl.multiple_of(core * half, half), half)]
        cross = rows_ref[pl.ds(pl.multiple_of(half + core * quarter, quarter), quarter)]
        out_ref[:, :half] = dot(block, block, LAST)
        out_ref[:, half:] = dot(top, cross, LAST)


def gram(place, rows):
    n, depth = rows.shape
    return pl.pallas_call(
        gram_kernel,
        out_shape=[f32(n // 2, n * 3 // 4)] * 2,
        in_specs=[SMEM, VMEM],
        out_specs=[VMEM] * 2,
        compiler_params=params(16),
        cost_estimate=cost(2 * n * n * depth, n * n),
        name="gram",
    )(place, rows)


def halves(x):
    high = x.astype(jnp.bfloat16)
    return high, (x - high.astype(jnp.float32)).astype(jnp.bfloat16)


def project_kernel(side, place_ref, rows_ref, trailing_ref, after_ref, out_ref):
    half = out_ref.shape[1]
    core = place_ref[1] if side == 0 else 1 - place_ref[1]
    out_ref[...] = dot(rows_ref[...], trailing_ref[:, pl.ds(pl.multiple_of(core * half, half), half)])


def project(side, place, rows, trailing, after):
    n, depth = rows.shape
    cols = trailing.shape[1]
    return pl.pallas_call(
        functools.partial(project_kernel, side),
        out_shape=f32(n, cols // 2),
        in_specs=[SMEM, VMEM, VMEM, ANYWHERE],
        out_specs=VMEM,
        compiler_params=params(16),
        cost_estimate=cost(n * cols * depth, n * depth + cols * depth + n * cols),
        name="project",
    )(place, rows, trailing, after)


def turn_kernel(rows_ref, high_ref, low_ref):
    high_ref[...], low_ref[...] = halves(rows_ref[...].T)


def turn(rows):
    n, depth = rows.shape
    steps = 4
    size = depth // steps
    part = pl.BlockSpec((size, n), lambda i: (i, 0))
    return pl.pallas_call(
        turn_kernel,
        grid=(steps,),
        out_shape=[jax.ShapeDtypeStruct((depth, n), jnp.bfloat16)] * 2,
        in_specs=[pl.BlockSpec((n, size), lambda i: (0, i))],
        out_specs=[part] * 2,
        compiler_params=params(16),
        cost_estimate=cost(n * depth, 2 * n * depth),
        name="turn",
    )(rows)


def spread_kernel(parts_ref, after_ref, out_ref):
    out_ref[...] = jnp.broadcast_to(jnp.sum(parts_ref[...], axis=0), out_ref.shape)


def spread(parts, after, copies):
    return pl.pallas_call(
        spread_kernel,
        out_shape=f32(copies, *parts.shape[1:]),
        in_specs=[VMEM, ANYWHERE],
        out_specs=VMEM,
        compiler_params=params(16),
        name="spread",
    )(parts, after)


def pack_kernel(parts_ref, mine_ref, theirs_ref, out_ref):
    copies, rows, _ = out_ref.shape
    width, cols = parts_ref.shape[2], mine_ref.shape[1]
    out_ref[:, :, :width] = jnp.broadcast_to(jnp.sum(parts_ref[...], axis=0), (copies, rows, width))
    total = (mine_ref[...] + theirs_ref[...]).reshape(copies, 2, rows, cols)
    out_ref[:, :, width : width + cols] = total[:, 0]
    out_ref[:, :, width + cols :] = total[:, 1]


def pack(parts, mine, theirs, copies):
    _, rows, width = parts.shape
    cols = mine.shape[1]
    return pl.pallas_call(
        pack_kernel,
        out_shape=f32(copies, rows, width + 2 * cols),
        in_specs=[VMEM] * 3,
        out_specs=VMEM,
        compiler_params=params(16),
        name="pack",
    )(parts, mine, theirs)


def unpack_kernel(parts_ref, after_ref, gram_ref, out_ref):
    width = gram_ref.shape[1]
    copies, rows, cols = out_ref.shape
    gram_ref[...] = parts_ref[:, :, :width].reshape(gram_ref.shape)
    for k in range(2):
        lo = width + k * cols
        total = jnp.sum(parts_ref[:, :, lo : lo + cols], axis=0)
        out_ref[:, k * rows // 2 : (k + 1) * rows // 2, :] = jnp.broadcast_to(total, (copies, rows // 2, cols))


def unpack(parts, after, width):
    copies, rows, both = parts.shape
    return pl.pallas_call(
        unpack_kernel,
        out_shape=[f32(copies * rows, width), f32(copies, 2 * rows, (both - width) // 2)],
        in_specs=[VMEM, ANYWHERE],
        out_specs=[VMEM] * 2,
        compiler_params=params(16),
        name="unpack",
    )(parts, after)


def wide(x):
    return jnp.broadcast_to(x, (GROUP, BLOCK))


def less(x, columns, rows):
    terms = [c * r for c, r in zip(columns, rows)]
    while len(terms) > 1:
        terms = [a + b for a, b in zip(terms[::2], terms[1::2])]
    return x - terms[0]


def invert_leaf(s):
    groups = len(s)
    lane = lax.broadcasted_iota(jnp.int32, (GROUP, BLOCK), 1)
    sub = lax.broadcasted_iota(jnp.int32, (GROUP, BLOCK), 0)
    out = []
    here = [wide(s[0][:, k : k + 1]) for k in range(GROUP)]
    for p in range(groups):
        at = GROUP * p
        last = p + 1 == groups
        columns = [[wide(s[q][:, at + k : at + k + 1]) for k in range(GROUP)] for q in range(p + 1, groups)]
        e = [[wide(here[k][i : i + 1, :]) for k in range(i + 1)] for i in range(GROUP)]
        inside = (lane >= at) & (lane < at + GROUP)
        own = jnp.where(inside, (lane == sub + at).astype(jnp.float32), s[p])
        for q in range(p + 1, groups):
            s[q] = jnp.where(inside, 0.0, s[q])
        rows = [wide(own[k : k + 1, :]) for k in range(GROUP)]
        near = [] if last else list(columns[0])
        inverse, factor = [None] * GROUP, {}
        for k in range(0, GROUP, 2):
            a, b, c = e[k][k], e[k + 1][k], e[k + 1][k + 1]
            inverse[k] = 1.0 / a
            inverse[k + 1] = a * (1.0 / (a * c - b * b))
            for j in (k, k + 1):
                for i in range(j + 1, GROUP):
                    f = factor[i, j] = e[i][j] * inverse[j]
                    for h in range(j + 1, i + 1):
                        e[i][h] = e[i][h] - f * e[h][j]
                    rows[i] = rows[i] - f * rows[j]
                    if near:
                        near[i] = near[i] - f * near[j]
        got = rows[0] * lax.rsqrt(e[0][0])
        for k in range(1, GROUP):
            got = jnp.where(sub == k, rows[k] * lax.rsqrt(e[k][k]), got)
        out.append(jnp.where(lane < at + GROUP, got, 0.0))
        if last:
            break
        scaled = [x * r for x, r in zip(near, inverse)]
        here = [wide(s[p + 1][:, at + GROUP + k : at + GROUP + k + 1]) for k in range(GROUP)]
        for k in range(GROUP):
            for j in range(GROUP):
                here[k] = here[k] - near[j] * wide(scaled[j][k : k + 1, :])
        rows = [x * r for x, r in zip(rows, inverse)]
        s[p + 1] = less(s[p + 1], near, rows)
        for k in range(GROUP - 1, -1, -1):
            for i in range(k + 1, GROUP):
                rows[k] = rows[k] - factor[i, k] * rows[i]
        for q in range(p + 2, groups):
            s[q] = less(s[q], columns[q - p - 1], rows)
    return out


def factor_kernel(place_ref, mine_ref, theirs_ref, upper_ref, inverse_ref, work, leaf):
    n = inverse_ref.shape[0]
    half, quarter = n // 2, n // 4
    steps = n // BLOCK
    row = lax.broadcasted_iota(jnp.int32, (n, n), 0)
    col = lax.broadcasted_iota(jnp.int32, (n, n), 1)
    for core, first_ref, second_ref in ((0, mine_ref, theirs_ref), (1, theirs_ref, mine_ref)):

        @pl.when(place_ref[1] == core)
        def _():
            work[:half, :half] = first_ref[:, :half]
            work[:half, half : half + quarter] = first_ref[:, half:]
            work[:half, half + quarter : n] = second_ref[:, half:]
            work[half:, half:n] = second_ref[:, :half]

    work[half:, :half] = jnp.zeros((half, half), jnp.float32)
    work[:, n:] = (row == col).astype(jnp.float32)
    square = (BLOCK, BLOCK)
    eye = lax.broadcasted_iota(jnp.int32, square, 0) == lax.broadcasted_iota(jnp.int32, square, 1)

    @pl.loop(0, steps)
    def _(p):
        at = pl.multiple_of(p * BLOCK, BLOCK)
        block = work[pl.ds(at, BLOCK), pl.ds(at, BLOCK)]
        scale = lax.rsqrt(jnp.sum(jnp.where(eye, block, 0.0), axis=0, keepdims=True))
        tall = jnp.sum(jnp.where(eye, jnp.broadcast_to(scale, square), 0.0), axis=1, keepdims=True)
        block = block * scale * tall
        groups = [slice(GROUP * q, GROUP * (q + 1)) for q in range(BLOCK // GROUP)]
        for group, rows in zip(groups, invert_leaf([block[group] for group in groups])):
            leaf[group, :] = rows * scale
        for k in range(steps):

            @pl.when(p == k)
            def _():
                lo, hi = k * BLOCK, (k + 1) * BLOCK
                end = n + hi
                panel = dot(leaf[...], work[lo:hi, lo:end])
                work[lo:hi, lo:end] = panel
                if hi < n:
                    work[hi:, hi:end] -= dot(panel[:, BLOCK : n - lo], panel[:, BLOCK:], FIRST)

    share = upper_ref.shape[0]
    offset = pl.multiple_of(place_ref[0], GROUP)
    row = offset + lax.broadcasted_iota(jnp.int32, (share, n), 0)
    col = lax.broadcasted_iota(jnp.int32, (share, n), 1)
    upper_ref[...] = jnp.where(row <= col, work[pl.ds(offset, share), :n], 0.0)
    inverse_ref[...] = work[:, n:]


def factor(place, mine, theirs, share):
    n = 2 * mine.shape[0]
    return pl.pallas_call(
        factor_kernel,
        out_shape=[f32(share, n), f32(n, n)],
        in_specs=[SMEM, VMEM, VMEM],
        out_specs=[VMEM] * 2,
        scratch_shapes=[pltpu.VMEM((n, 2 * n), jnp.float32), pltpu.VMEM((BLOCK, BLOCK), jnp.float32)],
        compiler_params=params(24),
        cost_estimate=cost(200 * n**3, 2 * n * n),
        name="factor",
    )(place, mine, theirs)


def solve_kernel(place_ref, inverse_ref, projected_ref, mine_ref, message_ref, whole):
    n = inverse_ref.shape[0]
    share = mine_ref.shape[0]
    half = n // 2
    whole[:half] = dot(inverse_ref[:half, :half], projected_ref[:half])
    whole[half:] = dot(inverse_ref[half:], projected_ref[...])
    message_ref[:half] = dot(inverse_ref[:, :half], whole[...], FIRST)
    message_ref[half:n] = dot(inverse_ref[half:, half:], whole[half:], FIRST)
    mine_ref[...] = whole[pl.ds(pl.multiple_of(place_ref[0], GROUP), share), :]
    message_ref[n:] = whole[pl.ds(pl.multiple_of(place_ref[2], GROUP), share), :]


def solve(place, inverse, projected, share):
    n, cols = projected.shape
    return pl.pallas_call(
        solve_kernel,
        out_shape=[f32(share, cols), f32(n + share, cols)],
        in_specs=[SMEM, VMEM, VMEM],
        out_specs=[VMEM] * 2,
        scratch_shapes=[pltpu.VMEM((n, cols), jnp.float32)],
        compiler_params=params(16),
        cost_estimate=cost(4 * n * n * cols, n * n + 2 * n * cols),
        name="solve",
    )(place, inverse, projected)


def product(high_ref, low_ref, weights):
    high, low = halves(weights)
    whole = lambda a, b: jnp.dot(a, b, preferred_element_type=jnp.float32)
    return whole(high_ref[...], low) + whole(low_ref[...], high) + whole(high_ref[...], high)


def first_half_kernel(place_ref, message_ref, high_ref, low_ref, trailing_ref, out_ref):
    out_ref[...] = trailing_ref[...] - product(high_ref, low_ref, message_ref[: high_ref.shape[1]])


def second_half_kernel(place_ref, message_ref, high_ref, low_ref, trailing_ref, mine_ref, done_ref, out_ref, coeff_ref):
    n = high_ref.shape[1]
    out_ref[...] = trailing_ref[...] - product(high_ref, low_ref, message_ref[:n])

    @pl.when(pl.program_id(0) == 0)
    def _():
        cols = mine_ref.shape[1]
        core = place_ref[1]
        coeff_ref[:, pl.ds(pl.multiple_of(core * cols, cols), cols)] = mine_ref[...]
        coeff_ref[:, pl.ds(pl.multiple_of((1 - core) * cols, cols), cols)] = message_ref[n:]


def half_specs(message, high, steps, side):
    size = high.shape[0] // steps
    cols = message.shape[1]
    part = pl.BlockSpec((size, high.shape[1]), lambda i, place: (i, 0))
    half = pl.BlockSpec((size, cols), lambda i, place: (i, place[1] if side == 0 else 1 - place[1]))
    return [pl.BlockSpec(message.shape, lambda i, place: (0, 0)), part, part, half], half


def first_half(place, message, high, low, trailing):
    steps = 2
    ins, half = half_specs(message, high, steps, 0)
    return pl.pallas_call(
        first_half_kernel,
        out_shape=f32(*trailing.shape),
        grid_spec=pltpu.PrefetchScalarGridSpec(num_scalar_prefetch=1, grid=(steps,), in_specs=ins, out_specs=half),
        compiler_params=params(24),
        cost_estimate=cost(high.size * trailing.shape[1], high.size + trailing.size),
        name="first_half",
    )(place, message, high, low, trailing)


def second_half(place, message, high, low, trailing, mine, done):
    steps = 2
    ins, half = half_specs(message, high, steps, 1)
    share, cols = mine.shape
    return pl.pallas_call(
        second_half_kernel,
        out_shape=[f32(*trailing.shape), f32(share, 2 * cols)],
        grid_spec=pltpu.PrefetchScalarGridSpec(
            num_scalar_prefetch=1,
            grid=(steps,),
            in_specs=[*ins, pl.BlockSpec((share, cols), lambda i, place: (0, 0)), ANYWHERE],
            out_specs=[half, pl.BlockSpec((share, 2 * cols), lambda i, place: (0, 0))],
        ),
        input_output_aliases={6: 0},
        compiler_params=params(24),
        cost_estimate=cost(high.size * trailing.shape[1], high.size + trailing.size),
        name="second_half",
    )(place, message, high, low, trailing, mine, done)


def swap(x):
    return lax.ppermute(x, "core", [(0, 1), (1, 0)])


def all_to_all(x, axes):
    return lax.all_to_all(x, axes, 0, 0)


def on_device(panel_block, trailing):
    depth, width = panel_block.shape
    groups, plane = lax.axis_size("col"), lax.axis_size(PLANE)
    n = width * groups
    share = n // lax.axis_size(ROWS)
    core = lax.axis_index("core")
    rank = lax.axis_index(ROWS)
    other = rank + (1 - 2 * core) * lax.axis_size("depth")
    place = jnp.stack([rank * share, core, other * share]).astype(jnp.int32)
    panel_rows = lax.all_gather(panel_block.T, "col", axis=0, tiled=True)
    few = panel_block.reshape(groups, depth // groups, width).transpose(0, 2, 1)
    few = all_to_all(few, "col").reshape(n, depth // groups)
    mine, theirs = gram(place, few)
    packed = (mine + swap(theirs)).reshape(plane, share, mine.shape[1])
    theirs = project(1, place, panel_rows, trailing, few)
    spread_out = spread(all_to_all(packed, PLANE), theirs, groups)
    packed = all_to_all(spread_out, "col")
    mine = project(0, place, panel_rows, trailing, spread_out)
    high, low = turn(panel_rows)
    both = all_to_all(pack(packed, mine, swap(theirs), plane), PLANE)
    gram_half, projected = unpack(both, high, packed.shape[2])
    projected = all_to_all(projected, PLANE).reshape(n, trailing.shape[1] // 2)
    upper_rows, inverse = factor(place, gram_half, swap(gram_half), share)
    mine, message = solve(place, inverse, projected, share)
    remainder = first_half(place, message, high, low, trailing)
    remainder, coeff_rows = second_half(place, swap(message), high, low, trailing, mine, remainder)
    return (upper_rows, coeff_rows, remainder)


def solution(mesh):
    rows, cols, depth = (mesh.shape[a] for a in ("row", "col", "depth"))
    split = Mesh(mesh.devices.reshape(rows // 2, 2, cols, depth), ("y", "core", "col", "depth"))
    return jax.shard_map(
        on_device,
        mesh=split,
        in_specs=(P(ROWS, "col"), P(ROWS, "col")),
        out_specs=(P(ROWS, None), P(ROWS, "col"), P(ROWS, "col")),
        check_vma=False,
    )
```

```python
import functools

import jax
import jax.numpy as jnp
from jax import lax
from jax.experimental import pallas as pl
from jax.experimental.pallas import tpu as pltpu
from jax.sharding import Mesh, PartitionSpec as P

BLOCK = 128
GROUP = 8
CHUNKS = 4
PLANE = ("y", "depth")
ROWS = ("y", "core", "depth")
VMEM = pl.BlockSpec(memory_space=pltpu.VMEM)
SMEM = pl.BlockSpec(memory_space=pltpu.SMEM)
ANYWHERE = pl.BlockSpec(memory_space=pl.ANY)
HBM = pl.BlockSpec(memory_space=pltpu.HBM)
HOPS = (0, 1, 2, -1, -2, 3, 4, -3)
EARLY = 5
NEAR = (0, 1, 2, 3, 4)
LAST = ((1,), (1,))
FIRST = ((0,), (0,))


def dot(a, b, contract=((1,), (0,))):
    return lax.dot_general(
        a, b, (contract, ((), ())), precision=lax.Precision.HIGHEST, preferred_element_type=jnp.float32
    )


def f32(*shape):
    return jax.ShapeDtypeStruct(shape, jnp.float32)


def outside(x):
    return pltpu.with_memory_space_constraint(x, pltpu.HBM)


def params(mib):
    return pltpu.CompilerParams(vmem_limit_bytes=mib * 2**20)


def cost(flops, values):
    return pl.CostEstimate(flops=flops, bytes_accessed=4 * values, transcendentals=0)


def halves(x):
    high = x.astype(jnp.bfloat16)
    return high, (x - high.astype(jnp.float32)).astype(jnp.bfloat16)


def fetch(pairs, sems):
    copies = [pltpu.make_async_copy(source, target, sems.at[k]) for k, (source, target) in enumerate(pairs)]
    for copy in copies:
        copy.start()
    return copies


def wait(copies):
    for copy in copies:
        copy.wait()


def join(piece_refs, rows_ref, first=0):
    width = piece_refs[0].shape[0]
    for k, piece_ref in enumerate(piece_refs[first:], first):
        rows_ref[k * width : (k + 1) * width] = piece_ref[...]


def sides(place_ref, theirs_ref, mine_ref):
    return (theirs_ref, 1 - place_ref[1]), (mine_ref, place_ref[1])


def half_of(ref, core):
    half = ref.shape[1] // 2
    return pl.ds(pl.multiple_of(core * half, half), half)


def early_kernel(place_ref, trailing_ref, *refs):
    *piece_refs, mine_ref, theirs_ref, rows, whole, sems = refs
    width = piece_refs[0].shape[0]
    n = rows.shape[0]
    size = whole.shape[0] // CHUNKS
    spans = [slice(k * size, (k + 1) * size) for k in range(CHUNKS)]
    copies = fetch([(piece_refs[0], rows.at[:width])] + [(trailing_ref.at[at], whole.at[at]) for at in spans], sems)
    join(piece_refs, rows, 1)
    copies[0].wait()
    for at, copy in zip(spans, copies[1:]):
        copy.wait()
        for out_ref, core in sides(place_ref, theirs_ref, mine_ref):
            product = dot(rows[:, at], whole[at, half_of(whole, core)])
            out_ref[...] = product if at.start == 0 else out_ref[...] + product


def early_products(place, pieces, trailing):
    depth, cols = trailing.shape
    n = sum(piece.shape[0] for piece in pieces)
    return pl.pallas_call(
        early_kernel,
        out_shape=[f32(n, cols // 2)] * 2,
        in_specs=[SMEM, HBM, HBM] + [VMEM] * (len(pieces) - 1),
        out_specs=[VMEM] * 2,
        scratch_shapes=[
            pltpu.VMEM((n, depth), jnp.float32),
            pltpu.VMEM((depth, cols), jnp.float32),
            pltpu.SemaphoreType.DMA((1 + CHUNKS,)),
        ],
        compiler_params=params(12),
        cost_estimate=cost(2 * n * cols * depth, n * depth + cols * depth + n * cols),
        name="early_products",
    )(place, outside(trailing), outside(pieces[0]), *pieces[1:])


def late_kernel(place_ref, trailing_ref, *refs):
    *piece_refs, mine_ref, theirs_ref, rows, gram_ref = refs
    width = piece_refs[0].shape[0]
    first = EARLY * width
    n = (len(HOPS) - EARLY) * width
    join(piece_refs, rows)
    for out_ref, core in sides(place_ref, theirs_ref, mine_ref):
        out_ref[:n] = dot(rows[first:], trailing_ref[:, half_of(trailing_ref, core)])
    own = rows[:width]
    gram_ref[:, : 3 * width] = dot(own, rows[: 3 * width], LAST)
    gram_ref[:, 3 * width : 5 * width] = dot(own, rows[first : first + 2 * width], LAST)
    gram_ref[:, 5 * width :] = jnp.zeros((width, gram_ref.shape[1] - 5 * width), jnp.float32)
    few = width // 2
    for out_ref, core in sides(place_ref, theirs_ref, mine_ref):
        span = pl.ds(pl.multiple_of(core * few, few), few)
        out_ref[n : n + few] = gram_ref[span, : 2 * BLOCK]
        out_ref[n + few :, :BLOCK] = gram_ref[span, 2 * BLOCK :]
        out_ref[n + few :, BLOCK:] = jnp.zeros((few, BLOCK), jnp.float32)


def late_products(place, pieces, trailing):
    depth, cols = trailing.shape
    width = pieces[0].shape[0]
    n = (len(HOPS) - EARLY) * width
    return pl.pallas_call(
        late_kernel,
        out_shape=[f32(n + width, cols // 2)] * 2,
        in_specs=[SMEM] + [VMEM] * (1 + len(pieces)),
        out_specs=[VMEM] * 2,
        scratch_shapes=[
            pltpu.VMEM((len(pieces) * width, depth), jnp.float32),
            pltpu.VMEM((width, 3 * BLOCK), jnp.float32),
        ],
        compiler_params=params(12),
        cost_estimate=cost(2 * n * cols * depth, n * depth + cols * depth + n * cols),
        name="late_products",
    )(place, trailing, *pieces)


def turn_kernel(*refs):
    *piece_refs, high_ref, low_ref, rows = refs
    join(piece_refs, rows)
    high_ref[...], low_ref[...] = halves(rows[...].T)


def turn(pieces):
    width, depth = pieces[0].shape
    n = width * len(pieces)
    return pl.pallas_call(
        turn_kernel,
        out_shape=[jax.ShapeDtypeStruct((depth, n), jnp.bfloat16)] * 2,
        in_specs=[VMEM] * len(pieces),
        out_specs=[VMEM] * 2,
        scratch_shapes=[pltpu.VMEM((n, depth), jnp.float32)],
        compiler_params=params(12),
        cost_estimate=cost(n * depth, 2 * n * depth),
        name="turn",
    )(*pieces)


def pack_kernel(early_ref, early_more_ref, late_ref, late_more_ref, out_ref):
    copies = out_ref.shape[0]
    rows, cols = GROUP, early_ref.shape[1]
    first = early_ref.shape[0] // (2 * rows)
    n = (copies - first) * 2 * rows
    for at, total in (
        (slice(0, first), early_ref[...] + early_more_ref[...]),
        (slice(first, copies), late_ref[:n] + late_more_ref[:n]),
    ):
        total = total.reshape(-1, 2, rows, cols)
        out_ref[at, :, :cols] = total[:, 0]
        out_ref[at, :, cols : 2 * cols] = total[:, 1]
    few = (late_ref.shape[0] - n) // 2
    part = late_ref[n:] + late_more_ref[n:]
    out_ref[:, 0, 2 * cols :] = part[:few, :BLOCK]
    out_ref[:, 1, 2 * cols :] = part[:few, BLOCK:]
    out_ref[:, 2, 2 * cols :] = part[few:, :BLOCK]
    for k in range(3, rows):
        out_ref[:, k, 2 * cols :] = part[few:, BLOCK:]


def pack(early, early_more, late, late_more, copies):
    cols = early.shape[1]
    return pl.pallas_call(
        pack_kernel,
        out_shape=f32(copies, GROUP, 2 * cols + BLOCK),
        in_specs=[VMEM] * 4,
        out_specs=VMEM,
        compiler_params=params(12),
        name="pack",
    )(early, early_more, late, late_more)


def unpack_kernel(parts_ref, after_ref, gram_ref, out_ref):
    copies, rows, cols = out_ref.shape
    for k in range(2):
        total = jnp.sum(parts_ref[:, :, k * cols : (k + 1) * cols], axis=0)
        out_ref[:, k * rows // 2 : (k + 1) * rows // 2, :] = jnp.broadcast_to(total, (copies, rows // 2, cols))
    gram_ref[...] = jnp.broadcast_to(jnp.sum(parts_ref[:, :, 2 * cols :], axis=0), gram_ref.shape)


def unpack(parts, after, groups):
    copies, rows, lanes = parts.shape
    return pl.pallas_call(
        unpack_kernel,
        out_shape=[f32(groups, rows, BLOCK), f32(copies, 2 * rows, (lanes - BLOCK) // 2)],
        in_specs=[VMEM, ANYWHERE],
        out_specs=[VMEM] * 2,
        compiler_params=params(12),
        name="unpack",
    )(parts, after)


def spread_kernel(parts_ref, out_ref):
    for k in range(parts_ref.shape[0]):
        out_ref[:, 3 * k : 3 * k + 3, :] = jnp.broadcast_to(parts_ref[k, :3], (out_ref.shape[0], 3, BLOCK))


def spread(parts, copies):
    groups = parts.shape[0]
    return pl.pallas_call(
        spread_kernel,
        out_shape=f32(copies, 3 * groups, BLOCK),
        in_specs=[VMEM],
        out_specs=VMEM,
        compiler_params=params(12),
        name="spread",
    )(parts)


def wide(x):
    return jnp.broadcast_to(x, (GROUP, BLOCK))


def less(x, columns, rows):
    terms = [c * r for c, r in zip(columns, rows)]
    while len(terms) > 1:
        terms = [a + b for a, b in zip(terms[::2], terms[1::2])]
    return x - terms[0]


def invert_leaf(s):
    groups = len(s)
    lane = lax.broadcasted_iota(jnp.int32, (GROUP, BLOCK), 1)
    sub = lax.broadcasted_iota(jnp.int32, (GROUP, BLOCK), 0)
    out = []
    here = [wide(s[0][:, k : k + 1]) for k in range(GROUP)]
    for p in range(groups):
        at = GROUP * p
        last = p + 1 == groups
        columns = [[wide(s[q][:, at + k : at + k + 1]) for k in range(GROUP)] for q in range(p + 1, groups)]
        e = [[wide(here[k][i : i + 1, :]) for k in range(i + 1)] for i in range(GROUP)]
        inside = (lane >= at) & (lane < at + GROUP)
        own = jnp.where(inside, (lane == sub + at).astype(jnp.float32), s[p])
        for q in range(p + 1, groups):
            s[q] = jnp.where(inside, 0.0, s[q])
        rows = [wide(own[k : k + 1, :]) for k in range(GROUP)]
        near = [] if last else list(columns[0])
        inverse, factor = [None] * GROUP, {}
        for k in range(0, GROUP, 2):
            a, b, c = e[k][k], e[k + 1][k], e[k + 1][k + 1]
            inverse[k] = 1.0 / a
            inverse[k + 1] = a * (1.0 / (a * c - b * b))
            for j in (k, k + 1):
                for i in range(j + 1, GROUP):
                    f = factor[i, j] = e[i][j] * inverse[j]
                    for h in range(j + 1, i + 1):
                        e[i][h] = e[i][h] - f * e[h][j]
                    rows[i] = rows[i] - f * rows[j]
                    if near:
                        near[i] = near[i] - f * near[j]
        got = rows[0] * lax.rsqrt(e[0][0])
        for k in range(1, GROUP):
            got = jnp.where(sub == k, rows[k] * lax.rsqrt(e[k][k]), got)
        out.append(jnp.where(lane < at + GROUP, got, 0.0))
        if last:
            break
        scaled = [x * r for x, r in zip(near, inverse)]
        here = [wide(s[p + 1][:, at + GROUP + k : at + GROUP + k + 1]) for k in range(GROUP)]
        for k in range(GROUP):
            for j in range(GROUP):
                here[k] = here[k] - near[j] * wide(scaled[j][k : k + 1, :])
        rows = [x * r for x, r in zip(rows, inverse)]
        s[p + 1] = less(s[p + 1], near, rows)
        for k in range(GROUP - 1, -1, -1):
            for i in range(k + 1, GROUP):
                rows[k] = rows[k] - factor[i, k] * rows[i]
        for q in range(p + 2, groups):
            s[q] = less(s[q], columns[q - p - 1], rows)
    return out


def factor_kernel(place_ref, mine_ref, theirs_ref, upper_ref, inverse_ref, work, leaf, blocks, parts, in_sems, out_sems):
    n = inverse_ref.shape[0]
    steps = n // BLOCK
    core = place_ref[1]
    copies = fetch([(mine_ref, parts.at[core]), (theirs_ref, parts.at[1 - core])], in_sems)
    row = lax.broadcasted_iota(jnp.int32, (n, n), 0)
    col = lax.broadcasted_iota(jnp.int32, (n, n), 1)
    groups = len(HOPS)
    width = n // groups
    few = width // 2
    work[:, n:] = (row == col).astype(jnp.float32)
    wait(copies)
    for half in range(2):
        x = jnp.swapaxes(parts[half], 0, 1)
        for c in range(groups):
            for k in range(3):
                blocks[c, half * few : (half + 1) * few, k * BLOCK : (k + 1) * BLOCK] = x[3 * c + k]

    def block_of(a, b):
        hop = (b - a) % groups
        if hop in NEAR:
            return blocks[a, :, hop * width : (hop + 1) * width]
        return block_of(b, a).T

    for a in range(0, groups, 2):
        for b in range(a, groups, 2):
            top = jnp.concatenate([block_of(a, b), block_of(a, b + 1)], axis=1)
            bottom = jnp.concatenate([block_of(a + 1, b), block_of(a + 1, b + 1)], axis=1)
            work[a * width : (a + 2) * width, b * width : (b + 2) * width] = jnp.concatenate([top, bottom], axis=0)
        if a:
            work[a * width : (a + 2) * width, : a * width] = jnp.zeros((2 * width, a * width), jnp.float32)
    square = (BLOCK, BLOCK)
    eye = lax.broadcasted_iota(jnp.int32, square, 0) == lax.broadcasted_iota(jnp.int32, square, 1)

    def inverse_rows(k):
        at = slice(k * BLOCK, (k + 1) * BLOCK)
        return pltpu.make_async_copy(work.at[at, n:], inverse_ref.at[at], out_sems.at[k])

    @pl.loop(0, steps)
    def _(p):
        at = pl.multiple_of(p * BLOCK, BLOCK)
        block = work[pl.ds(at, BLOCK), pl.ds(at, BLOCK)]
        scale = lax.rsqrt(jnp.sum(jnp.where(eye, block, 0.0), axis=0, keepdims=True))
        tall = jnp.sum(jnp.where(eye, jnp.broadcast_to(scale, square), 0.0), axis=1, keepdims=True)
        block = block * scale * tall
        groups = [slice(GROUP * q, GROUP * (q + 1)) for q in range(BLOCK // GROUP)]
        for group, rows in zip(groups, invert_leaf([block[group] for group in groups])):
            leaf[group, :] = rows * scale
        for k in range(steps):

            @pl.when(p == k)
            def _():
                lo, hi = k * BLOCK, (k + 1) * BLOCK
                end = n + hi
                panel = dot(leaf[...], work[lo:hi, lo:end])
                work[lo:hi, lo:end] = panel
                if hi < n:
                    work[hi:, hi:end] -= dot(panel[:, BLOCK : n - lo], panel[:, BLOCK:], FIRST)
                inverse_rows(k).start()

    share = upper_ref.shape[0]
    offset = pl.multiple_of(place_ref[0], GROUP)
    row = offset + lax.broadcasted_iota(jnp.int32, (share, n), 0)
    col = lax.broadcasted_iota(jnp.int32, (share, n), 1)
    upper_ref[...] = jnp.where(row <= col, work[pl.ds(offset, share), :n], 0.0)
    wait([inverse_rows(k) for k in range(steps)])


def factor(place, mine, theirs, share, n):
    return pl.pallas_call(
        factor_kernel,
        out_shape=[f32(share, n), pltpu.HBM((n, n), jnp.float32)],
        in_specs=[SMEM, HBM, HBM],
        out_specs=[VMEM, HBM],
        scratch_shapes=[
            pltpu.VMEM((n, 2 * n), jnp.float32),
            pltpu.VMEM((BLOCK, BLOCK), jnp.float32),
            pltpu.VMEM((len(HOPS), n // len(HOPS), 3 * BLOCK), jnp.float32),
            pltpu.VMEM((2, *mine.shape), jnp.float32),
            pltpu.SemaphoreType.DMA((2,)),
            pltpu.SemaphoreType.DMA((n // BLOCK,)),
        ],
        compiler_params=params(12),
        cost_estimate=cost(200 * n**3, 2 * n * n),
        name="factor",
    )(place, outside(mine), outside(theirs))


def solve_kernel(place_ref, inverse_ref, projected_ref, mine_ref, message_ref, inverse, sorted_rows, whole, sems):
    n = inverse.shape[0]
    share = mine_ref.shape[0]
    half, width = n // 2, n // len(HOPS)
    here = [pl.ds(k * width, width) for k in range(len(HOPS))]
    there = [
        pl.ds(pl.multiple_of(lax.rem(place_ref[3] + hop + len(HOPS), len(HOPS)) * width, width), width) for hop in HOPS
    ]
    copies = fetch([(inverse_ref.at[:half], inverse.at[:half]), (inverse_ref.at[half:], inverse.at[half:])], sems)
    for a, b in zip(here, there):
        sorted_rows[b, :] = projected_ref[a, :]
    copies[0].wait()
    whole[:half] = dot(inverse[:half, :half], sorted_rows[:half])
    copies[1].wait()
    whole[half:] = dot(inverse[half:], sorted_rows[...])
    sorted_rows[:half] = dot(inverse[:, :half], whole[...], FIRST)
    sorted_rows[half:] = dot(inverse[half:, half:], whole[half:], FIRST)
    for a, b in zip(here, there):
        message_ref[a, :] = sorted_rows[b, :]
    mine_ref[...] = whole[pl.ds(pl.multiple_of(place_ref[0], GROUP), share), :]
    message_ref[n:] = whole[pl.ds(pl.multiple_of(place_ref[2], GROUP), share), :]


def solve(place, inverse, projected, share):
    n, cols = projected.shape
    return pl.pallas_call(
        solve_kernel,
        out_shape=[f32(share, cols), f32(n + share, cols)],
        in_specs=[SMEM, HBM, VMEM],
        out_specs=[VMEM] * 2,
        scratch_shapes=[
            pltpu.VMEM((n, n), jnp.float32),
            pltpu.VMEM((n, cols), jnp.float32),
            pltpu.VMEM((n, cols), jnp.float32),
            pltpu.SemaphoreType.DMA((2,)),
        ],
        compiler_params=params(12),
        cost_estimate=cost(4 * n * n * cols, n * n + 2 * n * cols),
        name="solve",
    )(place, outside(inverse), projected)


def product(high_ref, low_ref, weights):
    high, low = halves(weights)
    whole = lambda a, b: jnp.dot(a, b, preferred_element_type=jnp.float32)
    return whole(high_ref[...], low) + whole(low_ref[...], high) + whole(high_ref[...], high)


def first_half_kernel(place_ref, message_ref, high_ref, low_ref, trailing_ref, out_ref):
    out_ref[...] = trailing_ref[...] - product(high_ref, low_ref, message_ref[: high_ref.shape[1]])


def second_half_kernel(place_ref, message_ref, high_ref, low_ref, trailing_ref, mine_ref, done_ref, out_ref, coeff_ref):
    n = high_ref.shape[1]
    out_ref[...] = trailing_ref[...] - product(high_ref, low_ref, message_ref[:n])

    @pl.when(pl.program_id(0) == 0)
    def _():
        cols = mine_ref.shape[1]
        core = place_ref[1]
        coeff_ref[:, pl.ds(pl.multiple_of(core * cols, cols), cols)] = mine_ref[...]
        coeff_ref[:, pl.ds(pl.multiple_of((1 - core) * cols, cols), cols)] = message_ref[n:]


def half_specs(message, high, steps, side):
    size = high.shape[0] // steps
    cols = message.shape[1]
    part = pl.BlockSpec((size, high.shape[1]), lambda i, place: (i, 0))
    half = pl.BlockSpec((size, cols), lambda i, place: (i, place[1] if side == 0 else 1 - place[1]))
    return [pl.BlockSpec(message.shape, lambda i, place: (0, 0)), part, part, half], half


def first_half(place, message, high, low, trailing):
    steps = 2
    ins, half = half_specs(message, high, steps, 0)
    return pl.pallas_call(
        first_half_kernel,
        out_shape=f32(*trailing.shape),
        grid_spec=pltpu.PrefetchScalarGridSpec(num_scalar_prefetch=1, grid=(steps,), in_specs=ins, out_specs=half),
        compiler_params=params(12),
        cost_estimate=cost(high.size * trailing.shape[1], high.size + trailing.size),
        name="first_half",
    )(place, message, high, low, trailing)


def second_half(place, message, high, low, trailing, mine, done):
    steps = 2
    ins, half = half_specs(message, high, steps, 1)
    share, cols = mine.shape
    return pl.pallas_call(
        second_half_kernel,
        out_shape=[f32(*trailing.shape), f32(share, 2 * cols)],
        grid_spec=pltpu.PrefetchScalarGridSpec(
            num_scalar_prefetch=1,
            grid=(steps,),
            in_specs=[*ins, pl.BlockSpec((share, cols), lambda i, place: (0, 0)), ANYWHERE],
            out_specs=[half, pl.BlockSpec((share, 2 * cols), lambda i, place: (0, 0))],
        ),
        input_output_aliases={6: 0},
        compiler_params=params(12),
        cost_estimate=cost(high.size * trailing.shape[1], high.size + trailing.size),
        name="second_half",
    )(place, message, high, low, trailing, mine, done)


def ring(x, hops):
    size = lax.axis_size("col")
    got = {0: x}
    for hop in hops[1:]:
        step = 1 if hop > 0 else -1
        got[hop] = lax.ppermute(got[hop - step], "col", [(i, (i - step) % size) for i in range(size)])
    return [got[hop] for hop in hops]


def swap(x):
    return lax.ppermute(x, "core", [(0, 1), (1, 0)])


def all_to_all(x, axes):
    return lax.all_to_all(x, axes, 0, 0)


def on_device(panel_block, trailing):
    depth, width = panel_block.shape
    groups, plane = lax.axis_size("col"), lax.axis_size(PLANE)
    n = width * groups
    cols = trailing.shape[1]
    share = n // lax.axis_size(ROWS)
    core = lax.axis_index("core")
    rank = lax.axis_index(ROWS)
    other = rank + (1 - 2 * core) * lax.axis_size("depth")
    place = jnp.stack([rank * share, core, other * share, lax.axis_index("col")]).astype(jnp.int32)
    pieces = ring(panel_block.T, HOPS)
    early, theirs = early_products(place, pieces[:EARLY], trailing)
    early_more = swap(theirs)
    late, theirs = late_products(place, pieces, trailing)
    parts = all_to_all(pack(early, early_more, late, swap(theirs), plane), PLANE)
    high, low = turn(pieces)
    gram, projected = unpack(parts, high, groups)
    gram = all_to_all(spread(all_to_all(gram, "col"), plane), PLANE)
    projected = all_to_all(projected, PLANE).reshape(n, cols // 2)
    upper_rows, inverse = factor(place, gram, swap(gram), share, n)
    mine, message = solve(place, inverse, projected, share)
    remainder = first_half(place, message, high, low, trailing)
    remainder, coeff_rows = second_half(place, swap(message), high, low, trailing, mine, remainder)
    return (upper_rows, coeff_rows, remainder)


def solution(mesh):
    rows, cols, depth = (mesh.shape[a] for a in ("row", "col", "depth"))
    split = Mesh(mesh.devices.reshape(rows // 2, 2, cols, depth), ("y", "core", "col", "depth"))
    return jax.shard_map(
        on_device,
        mesh=split,
        in_specs=(P(ROWS, "col"), P(ROWS, "col")),
        out_specs=(P(ROWS, None), P(ROWS, "col"), P(ROWS, "col")),
        check_vma=False,
    )
```

```python
import functools

import jax
import jax.numpy as jnp
from jax import lax
from jax.experimental import pallas as pl
from jax.experimental.pallas import tpu as pltpu
from jax.sharding import Mesh, PartitionSpec as P

BLOCK = 128
GROUP = 8
CHUNKS = 2
PLANE = ("y", "depth")
ROWS = ("y", "core", "depth")
VMEM = pl.BlockSpec(memory_space=pltpu.VMEM)
SMEM = pl.BlockSpec(memory_space=pltpu.SMEM)
ANYWHERE = pl.BlockSpec(memory_space=pl.ANY)
HBM = pl.BlockSpec(memory_space=pltpu.HBM)
HOPS = (0, 1, 2, -1, -2, 3, 4, -3)
EARLY = 5
NEAR = (0, 1, 2, 3, 4)
LAST = ((1,), (1,))
FIRST = ((0,), (0,))


def dot(a, b, contract=((1,), (0,))):
    return lax.dot_general(
        a, b, (contract, ((), ())), precision=lax.Precision.HIGHEST, preferred_element_type=jnp.float32
    )


def halves(x):
    high = x.astype(jnp.bfloat16)
    return high, (x - high.astype(jnp.float32)).astype(jnp.bfloat16)


def short_dot(a, b, contract=((1,), (0,))):
    (a_high, a_low), (b_high, b_low) = halves(a), halves(b)
    whole = lambda x, y: lax.dot_general(x, y, (contract, ((), ())), preferred_element_type=jnp.float32)
    return whole(a_high, b_low) + whole(a_low, b_high) + whole(a_high, b_high)


def f32(*shape):
    return jax.ShapeDtypeStruct(shape, jnp.float32)


def outside(x):
    return pltpu.with_memory_space_constraint(x, pltpu.HBM)


def params(mib):
    return pltpu.CompilerParams(vmem_limit_bytes=mib * 2**20)


def cost(flops, values):
    return pl.CostEstimate(flops=flops, bytes_accessed=4 * values, transcendentals=0)


def fetch(pairs, sems):
    copies = [pltpu.make_async_copy(source, target, sems.at[k]) for k, (source, target) in enumerate(pairs)]
    for copy in copies:
        copy.start()
    return copies


def wait(copies):
    for copy in copies:
        copy.wait()


def join(piece_refs, rows_ref, first=0):
    width = piece_refs[0].shape[0]
    for k, piece_ref in enumerate(piece_refs[first:], first):
        rows_ref[k * width : (k + 1) * width] = piece_ref[...]


def sides(place_ref, theirs_ref, mine_ref):
    return (theirs_ref, 1 - place_ref[1]), (mine_ref, place_ref[1])


def half_of(ref, core):
    half = ref.shape[1] // 2
    return pl.ds(pl.multiple_of(core * half, half), half)


def early_kernel(place_ref, trailing_ref, *refs):
    *piece_refs, mine_ref, theirs_ref, rows, whole, sems = refs
    width = piece_refs[0].shape[0]
    n = rows.shape[0]
    size = whole.shape[0] // CHUNKS
    spans = [slice(k * size, (k + 1) * size) for k in range(CHUNKS)]
    copies = fetch([(piece_refs[0], rows.at[:width])] + [(trailing_ref.at[at], whole.at[at]) for at in spans], sems)
    join(piece_refs, rows, 1)
    copies[0].wait()
    for at, copy in zip(spans, copies[1:]):
        copy.wait()
        for out_ref, core in sides(place_ref, theirs_ref, mine_ref):
            product = short_dot(rows[:, at], whole[at, half_of(whole, core)])
            out_ref[...] = product if at.start == 0 else out_ref[...] + product


def early_products(place, pieces, trailing):
    depth, cols = trailing.shape
    n = sum(piece.shape[0] for piece in pieces)
    return pl.pallas_call(
        early_kernel,
        out_shape=[f32(n, cols // 2)] * 2,
        in_specs=[SMEM, HBM, HBM] + [VMEM] * (len(pieces) - 1),
        out_specs=[VMEM] * 2,
        scratch_shapes=[
            pltpu.VMEM((n, depth), jnp.float32),
            pltpu.VMEM((depth, cols), jnp.float32),
            pltpu.SemaphoreType.DMA((1 + CHUNKS,)),
        ],
        compiler_params=params(12),
        cost_estimate=cost(2 * n * cols * depth, n * depth + cols * depth + n * cols),
        name="early_products",
    )(place, outside(trailing), outside(pieces[0]), *pieces[1:])


def late_kernel(place_ref, trailing_ref, *refs):
    *piece_refs, mine_ref, theirs_ref, rows, gram_ref = refs
    width = piece_refs[0].shape[0]
    n = (len(HOPS) - EARLY) * width
    first = rows.shape[0] - n
    join(piece_refs, rows)
    for out_ref, core in sides(place_ref, theirs_ref, mine_ref):
        out_ref[:n] = short_dot(rows[first:], trailing_ref[:, half_of(trailing_ref, core)])
    own = rows[:width]
    gram_ref[:, : 5 * width] = dot(own, rows[: 5 * width], LAST)
    gram_ref[:, 5 * width :] = jnp.zeros((width, gram_ref.shape[1] - 5 * width), jnp.float32)
    few = width // 2
    for out_ref, core in sides(place_ref, theirs_ref, mine_ref):
        span = pl.ds(pl.multiple_of(core * few, few), few)
        out_ref[n : n + few] = gram_ref[span, : 2 * BLOCK]
        out_ref[n + few :, :BLOCK] = gram_ref[span, 2 * BLOCK :]
        out_ref[n + few :, BLOCK:] = jnp.zeros((few, BLOCK), jnp.float32)


def late_products(place, pieces, trailing):
    depth, cols = trailing.shape
    width = pieces[0].shape[0]
    n = (len(HOPS) - EARLY) * width
    return pl.pallas_call(
        late_kernel,
        out_shape=[f32(n + width, cols // 2)] * 2,
        in_specs=[SMEM] + [VMEM] * (1 + len(pieces)),
        out_specs=[VMEM] * 2,
        scratch_shapes=[
            pltpu.VMEM((len(pieces) * width, depth), jnp.float32),
            pltpu.VMEM((width, 3 * BLOCK), jnp.float32),
        ],
        compiler_params=params(12),
        cost_estimate=cost(2 * n * cols * depth, n * depth + cols * depth + n * cols),
        name="late_products",
    )(place, trailing, *pieces)


def turn_kernel(*refs):
    *piece_refs, high_ref, low_ref, rows = refs
    join(piece_refs, rows)
    high_ref[...], low_ref[...] = halves(rows[...].T)


def turn(pieces):
    width, depth = pieces[0].shape
    n = width * len(pieces)
    return pl.pallas_call(
        turn_kernel,
        out_shape=[jax.ShapeDtypeStruct((depth, n), jnp.bfloat16)] * 2,
        in_specs=[VMEM] * len(pieces),
        out_specs=[VMEM] * 2,
        scratch_shapes=[pltpu.VMEM((n, depth), jnp.float32)],
        compiler_params=params(12),
        cost_estimate=cost(n * depth, 2 * n * depth),
        name="turn",
    )(*pieces)


def pack_kernel(early_ref, early_more_ref, late_ref, late_more_ref, out_ref):
    copies = out_ref.shape[0]
    rows, cols = GROUP, early_ref.shape[1]
    first = early_ref.shape[0] // (2 * rows)
    n = (copies - first) * 2 * rows
    for at, total in (
        (slice(0, first), early_ref[...] + early_more_ref[...]),
        (slice(first, copies), late_ref[:n] + late_more_ref[:n]),
    ):
        total = total.reshape(-1, 2, rows, cols)
        out_ref[at, :, :cols] = total[:, 0]
        out_ref[at, :, cols : 2 * cols] = total[:, 1]
    few = (late_ref.shape[0] - n) // 2
    part = late_ref[n:] + late_more_ref[n:]
    out_ref[:, 0, 2 * cols :] = part[:few, :BLOCK]
    out_ref[:, 1, 2 * cols :] = part[:few, BLOCK:]
    out_ref[:, 2, 2 * cols :] = part[few:, :BLOCK]
    for k in range(3, rows):
        out_ref[:, k, 2 * cols :] = part[few:, BLOCK:]


def pack(early, early_more, late, late_more, copies):
    cols = early.shape[1]
    return pl.pallas_call(
        pack_kernel,
        out_shape=f32(copies, GROUP, 2 * cols + BLOCK),
        in_specs=[VMEM] * 4,
        out_specs=VMEM,
        compiler_params=params(12),
        name="pack",
    )(early, early_more, late, late_more)


def unpack_kernel(parts_ref, after_ref, gram_ref, out_ref):
    copies, rows, cols = out_ref.shape
    for k in range(2):
        total = jnp.sum(parts_ref[:, :, k * cols : (k + 1) * cols], axis=0)
        out_ref[:, k * rows // 2 : (k + 1) * rows // 2, :] = jnp.broadcast_to(total, (copies, rows // 2, cols))
    gram_ref[...] = jnp.broadcast_to(jnp.sum(parts_ref[:, :, 2 * cols :], axis=0), gram_ref.shape)


def unpack(parts, after, groups):
    copies, rows, lanes = parts.shape
    return pl.pallas_call(
        unpack_kernel,
        out_shape=[f32(groups, rows, BLOCK), f32(copies, 2 * rows, (lanes - BLOCK) // 2)],
        in_specs=[VMEM, ANYWHERE],
        out_specs=[VMEM] * 2,
        compiler_params=params(12),
        name="unpack",
    )(parts, after)


def spread_kernel(parts_ref, out_ref):
    for k in range(parts_ref.shape[0]):
        out_ref[:, 3 * k : 3 * k + 3, :] = jnp.broadcast_to(parts_ref[k, :3], (out_ref.shape[0], 3, BLOCK))


def spread(parts, copies):
    groups = parts.shape[0]
    return pl.pallas_call(
        spread_kernel,
        out_shape=f32(copies, 3 * groups, BLOCK),
        in_specs=[VMEM],
        out_specs=VMEM,
        compiler_params=params(12),
        name="spread",
    )(parts)


def wide(x):
    return jnp.broadcast_to(x, (GROUP, BLOCK))


def less(x, columns, rows):
    terms = [c * r for c, r in zip(columns, rows)]
    while len(terms) > 1:
        terms = [a + b for a, b in zip(terms[::2], terms[1::2])]
    return x - terms[0]


def invert_leaf(s):
    groups = len(s)
    lane = lax.broadcasted_iota(jnp.int32, (GROUP, BLOCK), 1)
    sub = lax.broadcasted_iota(jnp.int32, (GROUP, BLOCK), 0)
    out = []
    here = [wide(s[0][:, k : k + 1]) for k in range(GROUP)]
    for p in range(groups):
        at = GROUP * p
        last = p + 1 == groups
        columns = [[wide(s[q][:, at + k : at + k + 1]) for k in range(GROUP)] for q in range(p + 1, groups)]
        e = [[wide(here[k][i : i + 1, :]) for k in range(i + 1)] for i in range(GROUP)]
        inside = (lane >= at) & (lane < at + GROUP)
        own = jnp.where(inside, (lane == sub + at).astype(jnp.float32), s[p])
        for q in range(p + 1, groups):
            s[q] = jnp.where(inside, 0.0, s[q])
        rows = [wide(own[k : k + 1, :]) for k in range(GROUP)]
        near = [] if last else list(columns[0])
        inverse, factor = [None] * GROUP, {}
        for k in range(0, GROUP, 2):
            a, b, c = e[k][k], e[k + 1][k], e[k + 1][k + 1]
            inverse[k] = 1.0 / a
            inverse[k + 1] = a * (1.0 / (a * c - b * b))
            for j in (k, k + 1):
                for i in range(j + 1, GROUP):
                    f = factor[i, j] = e[i][j] * inverse[j]
                    for h in range(j + 1, i + 1):
                        e[i][h] = e[i][h] - f * e[h][j]
                    rows[i] = rows[i] - f * rows[j]
                    if near:
                        near[i] = near[i] - f * near[j]
        got = rows[0] * lax.rsqrt(e[0][0])
        for k in range(1, GROUP):
            got = jnp.where(sub == k, rows[k] * lax.rsqrt(e[k][k]), got)
        out.append(jnp.where(lane < at + GROUP, got, 0.0))
        if last:
            break
        scaled = [x * r for x, r in zip(near, inverse)]
        here = [wide(s[p + 1][:, at + GROUP + k : at + GROUP + k + 1]) for k in range(GROUP)]
        for k in range(GROUP):
            for j in range(GROUP):
                here[k] = here[k] - near[j] * wide(scaled[j][k : k + 1, :])
        rows = [x * r for x, r in zip(rows, inverse)]
        s[p + 1] = less(s[p + 1], near, rows)
        for k in range(GROUP - 1, -1, -1):
            for i in range(k + 1, GROUP):
                rows[k] = rows[k] - factor[i, k] * rows[i]
        for q in range(p + 2, groups):
            s[q] = less(s[q], columns[q - p - 1], rows)
    return out


def factor_kernel(place_ref, mine_ref, theirs_ref, upper_ref, inverse_ref, work, leaf, blocks, parts, in_sems, out_sems):
    n = inverse_ref.shape[0]
    steps = n // BLOCK
    core = place_ref[1]
    copies = fetch([(mine_ref, parts.at[core]), (theirs_ref, parts.at[1 - core])], in_sems)
    row = lax.broadcasted_iota(jnp.int32, (n, n), 0)
    col = lax.broadcasted_iota(jnp.int32, (n, n), 1)
    groups = len(HOPS)
    width = n // groups
    few = width // 2
    work[:, n:] = (row == col).astype(jnp.float32)
    wait(copies)
    for half in range(2):
        x = jnp.swapaxes(parts[half], 0, 1)
        for c in range(groups):
            for k in range(3):
                blocks[c, half * few : (half + 1) * few, k * BLOCK : (k + 1) * BLOCK] = x[3 * c + k]

    def block_of(a, b):
        hop = (b - a) % groups
        if hop in NEAR:
            return blocks[a, :, hop * width : (hop + 1) * width]
        return block_of(b, a).T

    for a in range(0, groups, 2):
        for b in range(a, groups, 2):
            top = jnp.concatenate([block_of(a, b), block_of(a, b + 1)], axis=1)
            bottom = jnp.concatenate([block_of(a + 1, b), block_of(a + 1, b + 1)], axis=1)
            work[a * width : (a + 2) * width, b * width : (b + 2) * width] = jnp.concatenate([top, bottom], axis=0)
        if a:
            work[a * width : (a + 2) * width, : a * width] = jnp.zeros((2 * width, a * width), jnp.float32)
    square = (BLOCK, BLOCK)
    eye = lax.broadcasted_iota(jnp.int32, square, 0) == lax.broadcasted_iota(jnp.int32, square, 1)

    def inverse_rows(k):
        at = slice(k * BLOCK, (k + 1) * BLOCK)
        return pltpu.make_async_copy(work.at[at, n:], inverse_ref.at[at], out_sems.at[k])

    @pl.loop(0, steps)
    def _(p):
        at = pl.multiple_of(p * BLOCK, BLOCK)
        block = work[pl.ds(at, BLOCK), pl.ds(at, BLOCK)]
        scale = lax.rsqrt(jnp.sum(jnp.where(eye, block, 0.0), axis=0, keepdims=True))
        tall = jnp.sum(jnp.where(eye, jnp.broadcast_to(scale, square), 0.0), axis=1, keepdims=True)
        block = block * scale * tall
        groups = [slice(GROUP * q, GROUP * (q + 1)) for q in range(BLOCK // GROUP)]
        for group, rows in zip(groups, invert_leaf([block[group] for group in groups])):
            leaf[group, :] = rows * scale
        for k in range(steps):

            @pl.when(p == k)
            def _():
                lo, hi = k * BLOCK, (k + 1) * BLOCK
                end = n + hi
                panel = dot(leaf[...], work[lo:hi, lo:end])
                work[lo:hi, lo:end] = panel
                if hi < n:
                    work[hi:, hi:end] -= dot(panel[:, BLOCK : n - lo], panel[:, BLOCK:], FIRST)
                inverse_rows(k).start()

    share = upper_ref.shape[0]
    offset = pl.multiple_of(place_ref[0], GROUP)
    row = offset + lax.broadcasted_iota(jnp.int32, (share, n), 0)
    col = lax.broadcasted_iota(jnp.int32, (share, n), 1)
    upper_ref[...] = jnp.where(row <= col, work[pl.ds(offset, share), :n], 0.0)
    wait([inverse_rows(k) for k in range(steps)])


def factor(place, mine, theirs, share, n):
    return pl.pallas_call(
        factor_kernel,
        out_shape=[f32(share, n), pltpu.HBM((n, n), jnp.float32)],
        in_specs=[SMEM, HBM, HBM],
        out_specs=[VMEM, HBM],
        scratch_shapes=[
            pltpu.VMEM((n, 2 * n), jnp.float32),
            pltpu.VMEM((BLOCK, BLOCK), jnp.float32),
            pltpu.VMEM((len(HOPS), n // len(HOPS), 3 * BLOCK), jnp.float32),
            pltpu.VMEM((2, *mine.shape), jnp.float32),
            pltpu.SemaphoreType.DMA((2,)),
            pltpu.SemaphoreType.DMA((n // BLOCK,)),
        ],
        compiler_params=params(12),
        cost_estimate=cost(200 * n**3, 2 * n * n),
        name="factor",
    )(place, outside(mine), outside(theirs))


def solve_kernel(place_ref, inverse_ref, projected_ref, mine_ref, message_ref, inverse, sorted_rows, whole, sems):
    n = inverse.shape[0]
    share = mine_ref.shape[0]
    half, width = n // 2, n // len(HOPS)
    here = [pl.ds(k * width, width) for k in range(len(HOPS))]
    there = [
        pl.ds(pl.multiple_of(lax.rem(place_ref[3] + hop + len(HOPS), len(HOPS)) * width, width), width) for hop in HOPS
    ]
    copies = fetch([(inverse_ref.at[at], inverse.at[at]) for at in ((slice(0, half), slice(0, half)), slice(half, n))], sems)
    for a, b in zip(here, there):
        sorted_rows[b, :] = projected_ref[a, :]
    copies[0].wait()
    whole[:half] = dot(inverse[:half, :half], sorted_rows[:half])
    copies[1].wait()
    whole[half:] = dot(inverse[half:], sorted_rows[...])
    sorted_rows[:half] = short_dot(inverse[:, :half], whole[...], FIRST)
    sorted_rows[half:] = short_dot(inverse[half:, half:], whole[half:], FIRST)
    for a, b in zip(here, there):
        message_ref[a, :] = sorted_rows[b, :]
    mine_ref[...] = whole[pl.ds(pl.multiple_of(place_ref[0], GROUP), share), :]
    message_ref[n:] = whole[pl.ds(pl.multiple_of(place_ref[2], GROUP), share), :]


def solve(place, inverse, projected, share):
    n, cols = projected.shape
    return pl.pallas_call(
        solve_kernel,
        out_shape=[f32(share, cols), f32(n + share, cols)],
        in_specs=[SMEM, HBM, VMEM],
        out_specs=[VMEM] * 2,
        scratch_shapes=[
            pltpu.VMEM((n, n), jnp.float32),
            pltpu.VMEM((n, cols), jnp.float32),
            pltpu.VMEM((n, cols), jnp.float32),
            pltpu.SemaphoreType.DMA((2,)),
        ],
        compiler_params=params(12),
        cost_estimate=cost(4 * n * n * cols, n * n + 2 * n * cols),
        name="solve",
    )(place, outside(inverse), projected)


def product(high_ref, low_ref, weights):
    high, low = halves(weights)
    whole = lambda a, b: jnp.dot(a, b, preferred_element_type=jnp.float32)
    return whole(high_ref[...], low) + whole(low_ref[...], high) + whole(high_ref[...], high)


def first_half_kernel(place_ref, message_ref, high_ref, low_ref, trailing_ref, out_ref):
    out_ref[...] = trailing_ref[...] - product(high_ref, low_ref, message_ref[: high_ref.shape[1]])


def second_half_kernel(place_ref, message_ref, high_ref, low_ref, trailing_ref, mine_ref, done_ref, out_ref, coeff_ref):
    n = high_ref.shape[1]
    out_ref[...] = trailing_ref[...] - product(high_ref, low_ref, message_ref[:n])

    @pl.when(pl.program_id(0) == 0)
    def _():
        cols = mine_ref.shape[1]
        core = place_ref[1]
        coeff_ref[:, pl.ds(pl.multiple_of(core * cols, cols), cols)] = mine_ref[...]
        coeff_ref[:, pl.ds(pl.multiple_of((1 - core) * cols, cols), cols)] = message_ref[n:]


def half_specs(message, high, steps, side):
    size = high.shape[0] // steps
    cols = message.shape[1]
    part = pl.BlockSpec((size, high.shape[1]), lambda i, place: (i, 0))
    half = pl.BlockSpec((size, cols), lambda i, place: (i, place[1] if side == 0 else 1 - place[1]))
    return [pl.BlockSpec(message.shape, lambda i, place: (0, 0)), part, part, half], half


def first_half(place, message, high, low, trailing):
    steps = 2
    ins, half = half_specs(message, high, steps, 0)
    return pl.pallas_call(
        first_half_kernel,
        out_shape=f32(*trailing.shape),
        grid_spec=pltpu.PrefetchScalarGridSpec(num_scalar_prefetch=1, grid=(steps,), in_specs=ins, out_specs=half),
        compiler_params=params(12),
        cost_estimate=cost(high.size * trailing.shape[1], high.size + trailing.size),
        name="first_half",
    )(place, message, high, low, trailing)


def second_half(place, message, high, low, trailing, mine, done):
    steps = 2
    ins, half = half_specs(message, high, steps, 1)
    share, cols = mine.shape
    return pl.pallas_call(
        second_half_kernel,
        out_shape=[f32(*trailing.shape), f32(share, 2 * cols)],
        grid_spec=pltpu.PrefetchScalarGridSpec(
            num_scalar_prefetch=1,
            grid=(steps,),
            in_specs=[*ins, pl.BlockSpec((share, cols), lambda i, place: (0, 0)), ANYWHERE],
            out_specs=[half, pl.BlockSpec((share, 2 * cols), lambda i, place: (0, 0))],
        ),
        input_output_aliases={6: 0},
        compiler_params=params(12),
        cost_estimate=cost(high.size * trailing.shape[1], high.size + trailing.size),
        name="second_half",
    )(place, message, high, low, trailing, mine, done)


def ring(x, hops):
    size = lax.axis_size("col")
    got = {0: x}
    for hop in hops[1:]:
        step = 1 if hop > 0 else -1
        got[hop] = lax.ppermute(got[hop - step], "col", [(i, (i - step) % size) for i in range(size)])
    return [got[hop] for hop in hops]


def swap(x):
    return lax.ppermute(x, "core", [(0, 1), (1, 0)])


def all_to_all(x, axes):
    return lax.all_to_all(x, axes, 0, 0)


def on_device(panel_block, trailing):
    depth, width = panel_block.shape
    groups, plane = lax.axis_size("col"), lax.axis_size(PLANE)
    n = width * groups
    cols = trailing.shape[1]
    share = n // lax.axis_size(ROWS)
    core = lax.axis_index("core")
    rank = lax.axis_index(ROWS)
    other = rank + (1 - 2 * core) * lax.axis_size("depth")
    place = jnp.stack([rank * share, core, other * share, lax.axis_index("col")]).astype(jnp.int32)
    pieces = ring(panel_block.T, HOPS)
    early, theirs = early_products(place, pieces[:EARLY], trailing)
    early_more = swap(theirs)
    late, theirs = late_products(place, pieces[:3] + pieces[EARLY:], trailing)
    parts = all_to_all(pack(early, early_more, late, swap(theirs), plane), PLANE)
    high, low = turn(pieces)
    gram, projected = unpack(parts, high, groups)
    gram = all_to_all(spread(all_to_all(gram, "col"), plane), PLANE)
    projected = all_to_all(projected, PLANE).reshape(n, cols // 2)
    upper_rows, inverse = factor(place, gram, swap(gram), share, n)
    mine, message = solve(place, inverse, projected, share)
    remainder = first_half(place, message, high, low, trailing)
    remainder, coeff_rows = second_half(place, swap(message), high, low, trailing, mine, remainder)
    return (upper_rows, coeff_rows, remainder)


def solution(mesh):
    rows, cols, depth = (mesh.shape[a] for a in ("row", "col", "depth"))
    split = Mesh(mesh.devices.reshape(rows // 2, 2, cols, depth), ("y", "core", "col", "depth"))
    return jax.shard_map(
        on_device,
        mesh=split,
        in_specs=(P(ROWS, "col"), P(ROWS, "col")),
        out_specs=(P(ROWS, None), P(ROWS, "col"), P(ROWS, "col")),
        check_vma=False,
    )
```

```python
import functools

import jax
import jax.numpy as jnp
from jax import lax
from jax.experimental import pallas as pl
from jax.experimental.pallas import tpu as pltpu
from jax.sharding import Mesh, PartitionSpec as P

BLOCK = 128
GROUP = 8
CHUNKS = 2
PLANE = ("y", "depth")
ROWS = ("y", "core", "depth")
VMEM = pl.BlockSpec(memory_space=pltpu.VMEM)
SMEM = pl.BlockSpec(memory_space=pltpu.SMEM)
ANYWHERE = pl.BlockSpec(memory_space=pl.ANY)
HBM = pl.BlockSpec(memory_space=pltpu.HBM)
HOPS = (0, 1, 2, -1, -2, 3, 4, -3)
EARLY = 5
NEAR = (0, 1, 2, 3, 4)
LAST = ((1,), (1,))
FIRST = ((0,), (0,))


def dot(a, b, contract=((1,), (0,))):
    return lax.dot_general(
        a, b, (contract, ((), ())), precision=lax.Precision.HIGHEST, preferred_element_type=jnp.float32
    )


def halves(x):
    high = x.astype(jnp.bfloat16)
    return high, (x - high.astype(jnp.float32)).astype(jnp.bfloat16)


def short_dot(a, b, contract=((1,), (0,))):
    (a_high, a_low), (b_high, b_low) = halves(a), halves(b)
    whole = lambda x, y: lax.dot_general(x, y, (contract, ((), ())), preferred_element_type=jnp.float32)
    return whole(a_high, b_low) + whole(a_low, b_high) + whole(a_high, b_high)


def f32(*shape):
    return jax.ShapeDtypeStruct(shape, jnp.float32)


def outside(x):
    return pltpu.with_memory_space_constraint(x, pltpu.HBM)


def params(mib):
    return pltpu.CompilerParams(vmem_limit_bytes=mib * 2**20)


def cost(flops, values):
    return pl.CostEstimate(flops=flops, bytes_accessed=4 * values, transcendentals=0)


def fetch(pairs, sems):
    copies = [pltpu.make_async_copy(source, target, sems.at[k]) for k, (source, target) in enumerate(pairs)]
    for copy in copies:
        copy.start()
    return copies


def wait(copies):
    for copy in copies:
        copy.wait()


def join(piece_refs, rows_ref, first=0):
    width = piece_refs[0].shape[0]
    for k, piece_ref in enumerate(piece_refs[first:], first):
        rows_ref[k * width : (k + 1) * width] = piece_ref[...]


def sides(place_ref, theirs_ref, mine_ref):
    return (theirs_ref, 1 - place_ref[1]), (mine_ref, place_ref[1])


def half_of(ref, core):
    half = ref.shape[1] // 2
    return pl.ds(pl.multiple_of(core * half, half), half)


def early_kernel(place_ref, trailing_ref, *refs):
    *piece_refs, mine_ref, theirs_ref, rows, whole, sems = refs
    width = piece_refs[0].shape[0]
    n = rows.shape[0]
    size = whole.shape[0] // CHUNKS
    spans = [slice(k * size, (k + 1) * size) for k in range(CHUNKS)]
    copies = fetch([(piece_refs[0], rows.at[:width])] + [(trailing_ref.at[at], whole.at[at]) for at in spans], sems)
    join(piece_refs, rows, 1)
    copies[0].wait()
    for at, copy in zip(spans, copies[1:]):
        copy.wait()
        for out_ref, core in sides(place_ref, theirs_ref, mine_ref):
            product = short_dot(rows[:, at], whole[at, half_of(whole, core)])
            out_ref[...] = product if at.start == 0 else out_ref[...] + product


def early_products(place, pieces, trailing):
    depth, cols = trailing.shape
    n = sum(piece.shape[0] for piece in pieces)
    return pl.pallas_call(
        early_kernel,
        out_shape=[f32(n, cols // 2)] * 2,
        in_specs=[SMEM, HBM, HBM] + [VMEM] * (len(pieces) - 1),
        out_specs=[VMEM] * 2,
        scratch_shapes=[
            pltpu.VMEM((n, depth), jnp.float32),
            pltpu.VMEM((depth, cols), jnp.float32),
            pltpu.SemaphoreType.DMA((1 + CHUNKS,)),
        ],
        compiler_params=params(12),
        cost_estimate=cost(2 * n * cols * depth, n * depth + cols * depth + n * cols),
        name="early_products",
    )(place, outside(trailing), outside(pieces[0]), *pieces[1:])


def late_kernel(place_ref, trailing_ref, *refs):
    *piece_refs, mine_ref, theirs_ref, rows, gram_ref = refs
    width = piece_refs[0].shape[0]
    n = (len(HOPS) - EARLY) * width
    first = rows.shape[0] - n
    join(piece_refs, rows)
    for out_ref, core in sides(place_ref, theirs_ref, mine_ref):
        out_ref[:n] = short_dot(rows[first:], trailing_ref[:, half_of(trailing_ref, core)])
    own = rows[:width]
    gram_ref[:, : 5 * width] = dot(own, rows[: 5 * width], LAST)
    gram_ref[:, 5 * width :] = jnp.zeros((width, gram_ref.shape[1] - 5 * width), jnp.float32)
    few = width // 2
    for out_ref, core in sides(place_ref, theirs_ref, mine_ref):
        span = pl.ds(pl.multiple_of(core * few, few), few)
        out_ref[n : n + few] = gram_ref[span, : 2 * BLOCK]
        out_ref[n + few :, :BLOCK] = gram_ref[span, 2 * BLOCK :]
        out_ref[n + few :, BLOCK:] = jnp.zeros((few, BLOCK), jnp.float32)


def late_products(place, pieces, trailing):
    depth, cols = trailing.shape
    width = pieces[0].shape[0]
    n = (len(HOPS) - EARLY) * width
    return pl.pallas_call(
        late_kernel,
        out_shape=[f32(n + width, cols // 2)] * 2,
        in_specs=[SMEM] + [VMEM] * (1 + len(pieces)),
        out_specs=[VMEM] * 2,
        scratch_shapes=[
            pltpu.VMEM((len(pieces) * width, depth), jnp.float32),
            pltpu.VMEM((width, 3 * BLOCK), jnp.float32),
        ],
        compiler_params=params(12),
        cost_estimate=cost(2 * n * cols * depth, n * depth + cols * depth + n * cols),
        name="late_products",
    )(place, trailing, *pieces)


def turn_kernel(*refs):
    *piece_refs, high_ref, low_ref, rows = refs
    join(piece_refs, rows)
    high_ref[...], low_ref[...] = halves(rows[...].T)


def turn(pieces):
    width, depth = pieces[0].shape
    n = width * len(pieces)
    return pl.pallas_call(
        turn_kernel,
        out_shape=[jax.ShapeDtypeStruct((depth, n), jnp.bfloat16)] * 2,
        in_specs=[VMEM] * len(pieces),
        out_specs=[VMEM] * 2,
        scratch_shapes=[pltpu.VMEM((n, depth), jnp.float32)],
        compiler_params=params(12),
        cost_estimate=cost(n * depth, 2 * n * depth),
        name="turn",
    )(*pieces)


def pack_kernel(early_ref, early_more_ref, late_ref, late_more_ref, out_ref):
    copies = out_ref.shape[0]
    rows, cols = GROUP, early_ref.shape[1]
    first = early_ref.shape[0] // (2 * rows)
    n = (copies - first) * 2 * rows
    for at, total in (
        (slice(0, first), early_ref[...] + early_more_ref[...]),
        (slice(first, copies), late_ref[:n] + late_more_ref[:n]),
    ):
        total = total.reshape(-1, 2, rows, cols)
        out_ref[at, :, :cols] = total[:, 0]
        out_ref[at, :, cols : 2 * cols] = total[:, 1]
    few = (late_ref.shape[0] - n) // 2
    part = late_ref[n:] + late_more_ref[n:]
    out_ref[:, 0, 2 * cols :] = part[:few, :BLOCK]
    out_ref[:, 1, 2 * cols :] = part[:few, BLOCK:]
    out_ref[:, 2, 2 * cols :] = part[few:, :BLOCK]
    for k in range(3, rows):
        out_ref[:, k, 2 * cols :] = part[few:, BLOCK:]


def pack(early, early_more, late, late_more, copies):
    cols = early.shape[1]
    return pl.pallas_call(
        pack_kernel,
        out_shape=f32(copies, GROUP, 2 * cols + BLOCK),
        in_specs=[VMEM] * 4,
        out_specs=VMEM,
        compiler_params=params(12),
        name="pack",
    )(early, early_more, late, late_more)


def unpack_kernel(parts_ref, after_ref, gram_ref, out_ref):
    copies, rows, cols = out_ref.shape
    for k in range(2):
        total = jnp.sum(parts_ref[:, :, k * cols : (k + 1) * cols], axis=0)
        out_ref[:, k * rows // 2 : (k + 1) * rows // 2, :] = jnp.broadcast_to(total, (copies, rows // 2, cols))
    gram_ref[...] = jnp.broadcast_to(jnp.sum(parts_ref[:, :, 2 * cols :], axis=0), gram_ref.shape)


def unpack(parts, after, groups):
    copies, rows, lanes = parts.shape
    return pl.pallas_call(
        unpack_kernel,
        out_shape=[f32(groups, rows, BLOCK), f32(copies, 2 * rows, (lanes - BLOCK) // 2)],
        in_specs=[VMEM, ANYWHERE],
        out_specs=[VMEM] * 2,
        compiler_params=params(12),
        name="unpack",
    )(parts, after)


def spread_kernel(parts_ref, out_ref):
    for k in range(parts_ref.shape[0]):
        out_ref[:, 3 * k : 3 * k + 3, :] = jnp.broadcast_to(parts_ref[k, :3], (out_ref.shape[0], 3, BLOCK))


def spread(parts, copies):
    groups = parts.shape[0]
    return pl.pallas_call(
        spread_kernel,
        out_shape=f32(copies, 3 * groups, BLOCK),
        in_specs=[VMEM],
        out_specs=VMEM,
        compiler_params=params(12),
        name="spread",
    )(parts)


def wide(x):
    return jnp.broadcast_to(x, (GROUP, BLOCK))


def less(x, columns, rows):
    terms = [c * r for c, r in zip(columns, rows)]
    while len(terms) > 1:
        terms = [a + b for a, b in zip(terms[::2], terms[1::2])]
    return x - terms[0]


def invert_leaf(s):
    groups = len(s)
    lane = lax.broadcasted_iota(jnp.int32, (GROUP, BLOCK), 1)
    sub = lax.broadcasted_iota(jnp.int32, (GROUP, BLOCK), 0)
    out = []
    here = [wide(s[0][:, k : k + 1]) for k in range(GROUP)]
    for p in range(groups):
        at = GROUP * p
        last = p + 1 == groups
        columns = [[wide(s[q][:, at + k : at + k + 1]) for k in range(GROUP)] for q in range(p + 1, groups)]
        e = [[wide(here[k][i : i + 1, :]) for k in range(i + 1)] for i in range(GROUP)]
        inside = (lane >= at) & (lane < at + GROUP)
        own = jnp.where(inside, (lane == sub + at).astype(jnp.float32), s[p])
        for q in range(p + 1, groups):
            s[q] = jnp.where(inside, 0.0, s[q])
        rows = [wide(own[k : k + 1, :]) for k in range(GROUP)]
        near = [] if last else list(columns[0])
        inverse, factor = [None] * GROUP, {}
        for k in range(0, GROUP, 2):
            a, b, c = e[k][k], e[k + 1][k], e[k + 1][k + 1]
            inverse[k] = 1.0 / a
            inverse[k + 1] = a * (1.0 / (a * c - b * b))
            for j in (k, k + 1):
                for i in range(j + 1, GROUP):
                    f = factor[i, j] = e[i][j] * inverse[j]
                    for h in range(j + 1, i + 1):
                        e[i][h] = e[i][h] - f * e[h][j]
                    rows[i] = rows[i] - f * rows[j]
                    if near:
                        near[i] = near[i] - f * near[j]
        got = rows[0] * lax.rsqrt(e[0][0])
        for k in range(1, GROUP):
            got = jnp.where(sub == k, rows[k] * lax.rsqrt(e[k][k]), got)
        out.append(jnp.where(lane < at + GROUP, got, 0.0))
        if last:
            break
        scaled = [x * r for x, r in zip(near, inverse)]
        here = [wide(s[p + 1][:, at + GROUP + k : at + GROUP + k + 1]) for k in range(GROUP)]
        for k in range(GROUP):
            for j in range(GROUP):
                here[k] = here[k] - near[j] * wide(scaled[j][k : k + 1, :])
        rows = [x * r for x, r in zip(rows, inverse)]
        s[p + 1] = less(s[p + 1], near, rows)
        for k in range(GROUP - 1, -1, -1):
            for i in range(k + 1, GROUP):
                rows[k] = rows[k] - factor[i, k] * rows[i]
        for q in range(p + 2, groups):
            s[q] = less(s[q], columns[q - p - 1], rows)
    return out


def factor_kernel(place_ref, mine_ref, theirs_ref, upper_ref, inverse_ref, work, leaf, blocks, parts, in_sems, out_sems):
    n = inverse_ref.shape[0]
    steps = n // BLOCK
    core = place_ref[1]
    copies = fetch([(mine_ref, parts.at[core]), (theirs_ref, parts.at[1 - core])], in_sems)
    row = lax.broadcasted_iota(jnp.int32, (n, n), 0)
    col = lax.broadcasted_iota(jnp.int32, (n, n), 1)
    groups = len(HOPS)
    width = n // groups
    few = width // 2
    work[:, n:] = (row == col).astype(jnp.float32)
    wait(copies)
    for half in range(2):
        x = jnp.swapaxes(parts[half], 0, 1)
        for c in range(groups):
            for k in range(3):
                blocks[c, half * few : (half + 1) * few, k * BLOCK : (k + 1) * BLOCK] = x[3 * c + k]

    def block_of(a, b):
        hop = (b - a) % groups
        if hop in NEAR:
            return blocks[a, :, hop * width : (hop + 1) * width]
        return block_of(b, a).T

    for a in range(0, groups, 2):
        for b in range(a, groups, 2):
            top = jnp.concatenate([block_of(a, b), block_of(a, b + 1)], axis=1)
            bottom = jnp.concatenate([block_of(a + 1, b), block_of(a + 1, b + 1)], axis=1)
            work[a * width : (a + 2) * width, b * width : (b + 2) * width] = jnp.concatenate([top, bottom], axis=0)
        if a:
            work[a * width : (a + 2) * width, : a * width] = jnp.zeros((2 * width, a * width), jnp.float32)
    square = (BLOCK, BLOCK)
    eye = lax.broadcasted_iota(jnp.int32, square, 0) == lax.broadcasted_iota(jnp.int32, square, 1)

    def inverse_rows(k):
        at = slice(k * BLOCK, (k + 1) * BLOCK)
        return pltpu.make_async_copy(work.at[at, n:], inverse_ref.at[at], out_sems.at[k])

    @pl.loop(0, steps)
    def _(p):
        at = pl.multiple_of(p * BLOCK, BLOCK)
        block = work[pl.ds(at, BLOCK), pl.ds(at, BLOCK)]
        scale = lax.rsqrt(jnp.sum(jnp.where(eye, block, 0.0), axis=0, keepdims=True))
        tall = jnp.sum(jnp.where(eye, jnp.broadcast_to(scale, square), 0.0), axis=1, keepdims=True)
        block = block * scale * tall
        groups = [slice(GROUP * q, GROUP * (q + 1)) for q in range(BLOCK // GROUP)]
        for group, rows in zip(groups, invert_leaf([block[group] for group in groups])):
            leaf[group, :] = rows * scale
        for k in range(steps):

            @pl.when(p == k)
            def _():
                lo, hi = k * BLOCK, (k + 1) * BLOCK
                end = n + hi
                panel = dot(leaf[...], work[lo:hi, lo:end])
                work[lo:hi, lo:end] = panel
                if hi < n:
                    work[hi:, hi:end] -= dot(panel[:, BLOCK : n - lo], panel[:, BLOCK:], FIRST)
                inverse_rows(k).start()

    share = upper_ref.shape[0]
    offset = pl.multiple_of(place_ref[0], GROUP)
    row = offset + lax.broadcasted_iota(jnp.int32, (share, n), 0)
    col = lax.broadcasted_iota(jnp.int32, (share, n), 1)
    upper_ref[...] = jnp.where(row <= col, work[pl.ds(offset, share), :n], 0.0)
    wait([inverse_rows(k) for k in range(steps)])


def factor(place, mine, theirs, share, n):
    return pl.pallas_call(
        factor_kernel,
        out_shape=[f32(share, n), pltpu.HBM((n, n), jnp.float32)],
        in_specs=[SMEM, HBM, HBM],
        out_specs=[VMEM, HBM],
        scratch_shapes=[
            pltpu.VMEM((n, 2 * n), jnp.float32),
            pltpu.VMEM((BLOCK, BLOCK), jnp.float32),
            pltpu.VMEM((len(HOPS), n // len(HOPS), 3 * BLOCK), jnp.float32),
            pltpu.VMEM((2, *mine.shape), jnp.float32),
            pltpu.SemaphoreType.DMA((2,)),
            pltpu.SemaphoreType.DMA((n // BLOCK,)),
        ],
        compiler_params=params(12),
        cost_estimate=cost(200 * n**3, 2 * n * n),
        name="factor",
    )(place, outside(mine), outside(theirs))


def solve_kernel(place_ref, inverse_ref, projected_ref, mine_ref, message_ref, inverse, sorted_rows, whole, sems):
    n = inverse.shape[0]
    share = mine_ref.shape[0]
    half, width = n // 2, n // len(HOPS)
    here = [pl.ds(k * width, width) for k in range(len(HOPS))]
    there = [
        pl.ds(pl.multiple_of(lax.rem(place_ref[3] + hop + len(HOPS), len(HOPS)) * width, width), width) for hop in HOPS
    ]
    blocks = [(slice(0, half), slice(0, half)), slice(half, n)]
    copies = fetch(
        [(inverse_ref.at[at], inverse.at[at]) for at in blocks]
        + [(projected_ref.at[a], sorted_rows.at[b]) for a, b in zip(here, there)],
        sems,
    )
    wait(copies[2:])
    copies[0].wait()
    whole[:half] = dot(inverse[:half, :half], sorted_rows[:half])
    copies[1].wait()
    whole[half:] = dot(inverse[half:], sorted_rows[...])
    sorted_rows[:half] = short_dot(inverse[:, :half], whole[...], FIRST)
    sorted_rows[half:] = short_dot(inverse[half:, half:], whole[half:], FIRST)
    for a, b in zip(here, there):
        message_ref[a, :] = sorted_rows[b, :]
    mine_ref[...] = whole[pl.ds(pl.multiple_of(place_ref[0], GROUP), share), :]
    message_ref[n:] = whole[pl.ds(pl.multiple_of(place_ref[2], GROUP), share), :]


def solve(place, inverse, projected, share):
    n, cols = projected.shape
    return pl.pallas_call(
        solve_kernel,
        out_shape=[f32(share, cols), f32(n + share, cols)],
        in_specs=[SMEM, HBM, HBM],
        out_specs=[VMEM] * 2,
        scratch_shapes=[
            pltpu.VMEM((n, n), jnp.float32),
            pltpu.VMEM((n, cols), jnp.float32),
            pltpu.VMEM((n, cols), jnp.float32),
            pltpu.SemaphoreType.DMA((2 + len(HOPS),)),
        ],
        compiler_params=params(12),
        cost_estimate=cost(4 * n * n * cols, n * n + 2 * n * cols),
        name="solve",
    )(place, outside(inverse), outside(projected))


def product(high_ref, low_ref, weights):
    high, low = halves(weights)
    whole = lambda a, b: jnp.dot(a, b, preferred_element_type=jnp.float32)
    return whole(high_ref[...], low) + whole(low_ref[...], high) + whole(high_ref[...], high)


def first_half_kernel(place_ref, message_ref, high_ref, low_ref, trailing_ref, out_ref):
    out_ref[...] = trailing_ref[...] - product(high_ref, low_ref, message_ref[: high_ref.shape[1]])


def second_half_kernel(place_ref, message_ref, high_ref, low_ref, trailing_ref, mine_ref, done_ref, out_ref, coeff_ref):
    n = high_ref.shape[1]
    out_ref[...] = trailing_ref[...] - product(high_ref, low_ref, message_ref[:n])

    @pl.when(pl.program_id(0) == 0)
    def _():
        cols = mine_ref.shape[1]
        core = place_ref[1]
        coeff_ref[:, pl.ds(pl.multiple_of(core * cols, cols), cols)] = mine_ref[...]
        coeff_ref[:, pl.ds(pl.multiple_of((1 - core) * cols, cols), cols)] = message_ref[n:]


def half_specs(message, high, steps, side):
    size = high.shape[0] // steps
    cols = message.shape[1]
    part = pl.BlockSpec((size, high.shape[1]), lambda i, place: (i, 0))
    half = pl.BlockSpec((size, cols), lambda i, place: (i, place[1] if side == 0 else 1 - place[1]))
    return [pl.BlockSpec(message.shape, lambda i, place: (0, 0)), part, part, half], half


def first_half(place, message, high, low, trailing):
    steps = 2
    ins, half = half_specs(message, high, steps, 0)
    return pl.pallas_call(
        first_half_kernel,
        out_shape=f32(*trailing.shape),
        grid_spec=pltpu.PrefetchScalarGridSpec(num_scalar_prefetch=1, grid=(steps,), in_specs=ins, out_specs=half),
        compiler_params=params(12),
        cost_estimate=cost(high.size * trailing.shape[1], high.size + trailing.size),
        name="first_half",
    )(place, message, high, low, trailing)


def second_half(place, message, high, low, trailing, mine, done):
    steps = 2
    ins, half = half_specs(message, high, steps, 1)
    share, cols = mine.shape
    return pl.pallas_call(
        second_half_kernel,
        out_shape=[f32(*trailing.shape), f32(share, 2 * cols)],
        grid_spec=pltpu.PrefetchScalarGridSpec(
            num_scalar_prefetch=1,
            grid=(steps,),
            in_specs=[*ins, pl.BlockSpec((share, cols), lambda i, place: (0, 0)), ANYWHERE],
            out_specs=[half, pl.BlockSpec((share, 2 * cols), lambda i, place: (0, 0))],
        ),
        input_output_aliases={6: 0},
        compiler_params=params(12),
        cost_estimate=cost(high.size * trailing.shape[1], high.size + trailing.size),
        name="second_half",
    )(place, message, high, low, trailing, mine, done)


def ring(x, hops):
    size = lax.axis_size("col")
    got = {0: x}
    for hop in hops[1:]:
        step = 1 if hop > 0 else -1
        got[hop] = lax.ppermute(got[hop - step], "col", [(i, (i - step) % size) for i in range(size)])
    return [got[hop] for hop in hops]


def swap(x):
    return lax.ppermute(x, "core", [(0, 1), (1, 0)])


def all_to_all(x, axes):
    return lax.all_to_all(x, axes, 0, 0)


def on_device(panel_block, trailing):
    depth, width = panel_block.shape
    groups, plane = lax.axis_size("col"), lax.axis_size(PLANE)
    n = width * groups
    cols = trailing.shape[1]
    share = n // lax.axis_size(ROWS)
    core = lax.axis_index("core")
    rank = lax.axis_index(ROWS)
    other = rank + (1 - 2 * core) * lax.axis_size("depth")
    place = jnp.stack([rank * share, core, other * share, lax.axis_index("col")]).astype(jnp.int32)
    pieces = ring(panel_block.T, HOPS)
    early, theirs = early_products(place, pieces[:EARLY], trailing)
    early_more = swap(theirs)
    late, theirs = late_products(place, pieces[:3] + pieces[EARLY:], trailing)
    parts = all_to_all(pack(early, early_more, late, swap(theirs), plane), PLANE)
    high, low = turn(pieces)
    gram, projected = unpack(parts, high, groups)
    gram = all_to_all(spread(all_to_all(gram, "col"), plane), PLANE)
    projected = all_to_all(projected, PLANE).reshape(n, cols // 2)
    upper_rows, inverse = factor(place, gram, swap(gram), share, n)
    mine, message = solve(place, inverse, projected, share)
    remainder = first_half(place, message, high, low, trailing)
    remainder, coeff_rows = second_half(place, swap(message), high, low, trailing, mine, remainder)
    return (upper_rows, coeff_rows, remainder)


def solution(mesh):
    rows, cols, depth = (mesh.shape[a] for a in ("row", "col", "depth"))
    split = Mesh(mesh.devices.reshape(rows // 2, 2, cols, depth), ("y", "core", "col", "depth"))
    return jax.shard_map(
        on_device,
        mesh=split,
        in_specs=(P(ROWS, "col"), P(ROWS, "col")),
        out_specs=(P(ROWS, None), P(ROWS, "col"), P(ROWS, "col")),
        check_vma=False,
    )
```
